32 devices in a mesh: energy: 8 (over y, x, core), pair: 4 (over z).
Axes of the slice: x: 2, y: 2, z: 4, core: 2. Of those that a mesh axis runs over, the one named last changes fastest.
Arguments:
- green_less: bfloat16 [2, 8, 1024, 256], P(None, 'energy', 'pair'), may hold values from -6 to 6
- green_greater: bfloat16 [2, 8, 1024, 256], P(None, 'energy', 'pair'), may hold values from -6 to 6
- pair_blocks: int32 [4, 2], P('pair'), may hold values from 0 to 2, as said below
- onsite_scale: float32 [3], replicated, may hold values from 0.5 to 2
- coupling_scale: float32 [2], replicated, may hold values from 0.5 to 2
- coupling_mask: int32 [3, 3], replicated, may hold values 0 or 1
- onsite_block: bfloat16 [256, 256], replicated, may hold values from -0.375 to 0.375
- coupling_block: bfloat16 [256, 256], replicated, may hold values from -0.375 to 0.375
Outputs:
- screened: bfloat16 [2, 8, 1024, 256], P(None, 'energy', 'pair')
The draws below stay inside these ranges and needn't reach their ends.
Inputs may be any that keep to these rules, and one draw needn't show every extreme that they name: `pair_blocks`: for each s below 2, slot s holds (i, i + 1) or (i + 1, i) for some i, and slot s + 2 holds the same two blocks in reverse order; every i from 0 to 1 occurs in exactly one slot below 2.
All inputs are finite; a program needn't handle non-finite values.
Results may differ from the reference program's by a relative error of at most 0.012.
Values may be sent and summed in bfloat16 or wider, within the bound.
No kernel may reach another device: no remote copies, remote signals or barrier semaphores. Data moves between devices by JAX's collectives and lax.ppermute only.
A program may use at most 64 MiB of HBM per device.

```python
import math
import jax
import jax.numpy as jnp
from jax import lax

BLOCK = 256
NE = 8
SLOTS = 4
HALF = 2
NBLK = 3


def draw_pair_blocks(key, part):
    key = jax.random.fold_in(key, 11)
    order_key, flip_key = jax.random.split(key)
    order = jax.random.permutation(order_key, HALF).astype(jnp.int32)
    flips = jax.random.randint(flip_key, (HALF,), 0, 2).astype(jnp.int32)
    first = order + flips
    second = order + 1 - flips
    upper_rows = jnp.stack([first, second], axis=1)
    lower_rows = jnp.stack([second, first], axis=1)
    return jnp.concatenate([upper_rows, lower_rows], axis=0)


def set_ends(entries, rng, smallest, high):
    spot = [jax.random.randint(jax.random.fold_in(rng, axis), (), 0, length) for axis, length in enumerate(entries.shape)]
    widest = entries.shape.index(max(entries.shape))
    neighbour = spot[:widest] + [(spot[widest] + 1) % entries.shape[widest]] + spot[widest + 1:]
    return entries.at[tuple(spot)].set(smallest).at[tuple(neighbour)].set(high)


def level_of(rng, shape, cuts, low, high):
    gain = 1.0
    for axis_at, parts in cuts:
        steps = jax.random.uniform(jax.random.fold_in(jax.random.fold_in(rng, 6), axis_at), (parts,), jnp.float32, low / len(cuts), high / len(cuts))
        gain = gain * jnp.repeat(jnp.exp(steps), shape[axis_at] // parts).reshape((-1,) + (1,) * (len(shape) - 1 - axis_at))
    return gain


def gaussian(key, extent, deviation, reach, cuts=(), held_as=jnp.bfloat16):
    factor_of = level_of(key, extent, cuts, -0.22, 0.18) if cuts else 1.0
    entries = jax.random.normal(key, extent, jnp.float32) * deviation * factor_of
    return jnp.minimum(jnp.maximum(entries, -reach), reach).astype(held_as)


def setup_inputs(seed: int = 0) -> dict:
    arg_keys = jax.random.split(jax.random.key(seed), 9)
    return {
        "green_less": gaussian(arg_keys[0], (2, NE, SLOTS * BLOCK, BLOCK), 1.0, 6.0, ((1, 8), (2, 4))),
        "green_greater": gaussian(arg_keys[1], (2, NE, SLOTS * BLOCK, BLOCK), 1.0, 6.0, ((1, 8), (2, 4))),
        "pair_blocks": draw_pair_blocks(jax.random.fold_in(arg_keys[8], 71), 0),
        "onsite_scale": jnp.clip(jnp.exp(jax.random.uniform(arg_keys[3], (NBLK,), jnp.float32, math.log(0.5), math.log(2.0))), 0.5, 2.0),
        "coupling_scale": jnp.clip(jnp.exp(jax.random.uniform(arg_keys[4], (HALF,), jnp.float32, math.log(0.5), math.log(2.0))), 0.5, 2.0),
        "coupling_mask": set_ends((jax.random.randint(arg_keys[5], (NBLK, NBLK), 0, 4) < 3).astype(jnp.int32), jax.random.fold_in(arg_keys[5], 1), 0, 1),
        "onsite_block": gaussian(arg_keys[6], (BLOCK, BLOCK), BLOCK ** -0.5, 0.375),
        "coupling_block": gaussian(arg_keys[7], (BLOCK, BLOCK), BLOCK ** -0.5, 0.375),
    }


PRECISE = lax.Precision.HIGHEST


def fourier_tables(energies):
    length = 2 * energies
    frequency = jnp.arange(length, dtype=jnp.int32)
    energy_index = jnp.arange(energies, dtype=jnp.int32)
    phases = ((frequency[:, None] * energy_index[None, :]) % length).astype(jnp.float32) * (2.0 * math.pi / length)
    cosine = jnp.cos(phases)
    sine_table = jnp.sin(phases)
    forward = jnp.concatenate([cosine, sine_table], axis=0)
    top_rows = jnp.concatenate([cosine.T, -sine_table.T], axis=1)
    bottom_rows = jnp.concatenate([sine_table.T, cosine.T], axis=1)
    inverse = jnp.concatenate([top_rows, bottom_rows], axis=0) / length
    return forward, inverse


def transform(forward, real_part, imag_part, sign_flip):
    length = forward.shape[0] // 2
    real_spec = jnp.dot(forward, real_part, precision=PRECISE, preferred_element_type=jnp.float32)
    imag_spec = jnp.dot(forward, imag_part, precision=PRECISE, preferred_element_type=jnp.float32)
    out_real = real_spec[:length] + sign_flip * imag_spec[length:]
    out_imag = imag_spec[:length] - sign_flip * real_spec[length:]
    return out_real, out_imag


def spectrum(forward, element_block, sign_flip):
    flat = element_block.reshape(2, element_block.shape[1], -1).astype(jnp.float32)
    return transform(forward, flat[0], flat[1], sign_flip)


def multiply_spectra(less_spec, more_spec, inverse, energies):
    prod_real = less_spec[0] * more_spec[0] - less_spec[1] * more_spec[1]
    prod_imag = less_spec[0] * more_spec[1] + less_spec[1] * more_spec[0]
    lagged = jnp.dot(inverse, jnp.concatenate([prod_real, prod_imag], axis=0), precision=PRECISE, preferred_element_type=jnp.float32)
    factor = energies ** -0.5
    return jnp.stack([factor * lagged[energies:], -factor * lagged[:energies]]).astype(jnp.bfloat16)


def sandwich_exact(left_block, middle, right_block):
    inner_block = jnp.einsum('ij,cejk->ceik', left_block.astype(jnp.float32), middle.astype(jnp.float32), precision=PRECISE)
    inner_block = lax.optimization_barrier(inner_block.astype(jnp.bfloat16))
    return jnp.einsum('ceij,jk->ceik', inner_block.astype(jnp.float32), right_block.astype(jnp.float32), precision=PRECISE)


def reference(green_less, green_greater, pair_blocks, onsite_scale, coupling_scale, coupling_mask, onsite_block, coupling_block):
    lesser = green_less.reshape(2, NE, SLOTS, BLOCK, BLOCK)
    greater = green_greater.reshape(2, NE, SLOTS, BLOCK, BLOCK)
    forward, inverse = fourier_tables(NE)

    def one_slot(slot_index):
        less_slot = lax.dynamic_index_in_dim(lesser, slot_index, 2, keepdims=False)
        partner = ((slot_index + HALF) % SLOTS).astype(jnp.int32)
        mirror_slot = jnp.swapaxes(lax.dynamic_index_in_dim(greater, partner, 2, keepdims=False), 2, 3)
        less_spec = spectrum(forward, less_slot, 1.0)
        more_spec = spectrum(forward, mirror_slot, -1.0)
        return multiply_spectra(less_spec, more_spec, inverse, NE).reshape(2, NE, BLOCK, BLOCK)

    slot_range = jnp.arange(SLOTS, dtype=jnp.int32)
    polar_all = lax.map(one_slot, slot_range)

    def screen_slot(slot_index):
        polar_own = lax.optimization_barrier(polar_all[slot_index])
        partner = ((slot_index + HALF) % SLOTS).astype(jnp.int32)
        polar_other = lax.optimization_barrier(polar_all[partner])
        row_block = pair_blocks[slot_index, 0]
        col_block = pair_blocks[slot_index, 1]
        lower_block = jnp.minimum(row_block, col_block)
        onsite_factor = onsite_scale[row_block] * onsite_scale[col_block]
        mask_value = coupling_mask[lower_block, lower_block + 1].astype(jnp.float32)
        mirror_weight = mask_value * coupling_scale[lower_block] * coupling_scale[lower_block]
        coupling = jnp.where(row_block < col_block, coupling_block, coupling_block.T)
        own_term = onsite_factor * sandwich_exact(onsite_block, polar_own, onsite_block)
        other_term = lax.optimization_barrier((mirror_weight * sandwich_exact(coupling, polar_other, coupling)).astype(jnp.bfloat16))
        return (own_term + other_term.astype(jnp.float32)).astype(jnp.bfloat16)

    screened_all = lax.map(screen_slot, slot_range)
    return jnp.moveaxis(screened_all, 0, 2).reshape(2, NE, SLOTS * BLOCK, BLOCK)
```

```python
import functools

import jax
import jax.numpy as jnp
from jax import lax
from jax.experimental import pallas as pl
from jax.experimental.pallas import tpu as pltpu
from jax.sharding import Mesh
from jax.sharding import PartitionSpec as P

BF16 = jnp.bfloat16
F32 = jnp.float32
VMEM = pl.BlockSpec(memory_space=pltpu.VMEM)
SMEM = pl.BlockSpec(memory_space=pltpu.SMEM)


def run_kernel(body, outs, args, specs=None, scratch=(), flops=0):
    return pl.pallas_call(
        body,
        out_shape=[jax.ShapeDtypeStruct(shape, dtype) for shape, dtype in outs],
        in_specs=specs or [VMEM] * len(args),
        out_specs=[VMEM] * len(outs),
        scratch_shapes=list(scratch),
        compiler_params=pltpu.CompilerParams(vmem_limit_bytes=12 * 2**20),
        cost_estimate=pl.CostEstimate(flops=flops, bytes_accessed=2**19, transcendentals=0),
    )(*args)


def split_body(whole, away, keep):
    core = lax.axis_index("core")
    for part in range(2):
        away[:, part] = whole[part, :, 1 - core]
        keep[:, part] = whole[part, :, core]


def sort_body(keep, got, *routes):
    chip = lax.axis_index("chip")
    for step, route in enumerate(routes):
        route[0] = keep[chip ^ step]
        route[1] = got[chip ^ step]


def turn_body(less, turned):
    groups, _, rows, _ = turned.shape
    for part in range(2):
        flipped = less[part, 0].astype(F32).T.astype(BF16)
        for group in range(groups):
            turned[group, part] = flipped[group * rows : (group + 1) * rows]


def lag_body(*refs):
    less, routes = refs[0], refs[1:-4]
    own, away, keep, more = refs[-4:]
    energies, _, rows, width = less.shape
    chip, core = lax.axis_index("chip"), lax.axis_index("core")
    for step, route in enumerate(routes):
        first = 2 * (chip ^ step)
        more[first + core] = route[0]
        more[first + 1 - core] = route[1]
    factor = energies ** (-0.5)
    for top in range(0, rows, 16):
        for left in range(0, width, 128):
            at = (pl.ds(top, 16), pl.ds(left, 128))
            for lag in range(energies):
                real = jnp.zeros((16, 128), F32)
                imag = jnp.zeros((16, 128), F32)
                for late in range(lag, energies):
                    lr = less[(late, 0) + at].astype(F32)
                    li = less[(late, 1) + at].astype(F32)
                    mr = more[(late - lag, 0) + at].astype(F32)
                    mi = more[(late - lag, 1) + at].astype(F32)
                    real += lr * mr - li * mi
                    imag += lr * mi + li * mr
                own[(lag, 0) + at] = (factor * imag).astype(BF16)
                own[(lag, 1) + at] = (-factor * real).astype(BF16)
    for chip_at in range(energies // 2):
        away[chip_at] = own[2 * chip_at + 1 - core]
        keep[chip_at] = own[2 * chip_at + core]


def across(left, turned):
    return lax.dot_general(
        left, turned, (((1,), (1,)), ((), ())), preferred_element_type=F32
    ).astype(BF16)


def own_body(blocks, onsite_scale, coupling_scale, mask, own, onsite, link, term, coupling, weight):
    row, col = blocks[0, 0], blocks[0, 1]
    low = jnp.minimum(row, col)
    scale = onsite_scale[row] * onsite_scale[col]
    strength = coupling_scale[low]
    weight[...] = jnp.full(
        weight.shape, mask[low, low + 1].astype(F32) * strength * strength, F32
    )
    width = onsite.shape[0]
    for part in range(2):
        inner = across(onsite[...], own[:, part].reshape(width, width))
        term[part] = scale * jnp.dot(inner, onsite[...], preferred_element_type=F32)

    @pl.when(row < col)
    def _():
        coupling[...] = link[...]

    @pl.when(row >= col)
    def _():
        coupling[...] = link[...].astype(F32).T.astype(BF16)


def join_body(*refs):
    routes = refs[:-5]
    term, coupling, weight, out, other = refs[-5:]
    rows = routes[0].shape[2]
    chip, core = lax.axis_index("chip"), lax.axis_index("core")
    for step, route in enumerate(routes):
        first = 2 * (chip ^ step)
        for part in range(2):
            other[part, pl.ds(pl.multiple_of((first + core) * rows, rows), rows)] = route[0, part]
            other[part, pl.ds(pl.multiple_of((first + 1 - core) * rows, rows), rows)] = route[1, part]
    for part in range(2):
        inner = across(coupling[...], other[part])
        mirrored = jnp.dot(inner, coupling[...], preferred_element_type=F32)
        mirrored = (weight[0, 0] * mirrored).astype(BF16).astype(F32)
        out[part, 0] = (term[part] + mirrored).astype(BF16)


def on_device(
    green_less,
    green_greater,
    pair_blocks,
    onsite_scale,
    coupling_scale,
    coupling_mask,
    onsite_block,
    coupling_block,
):
    chips = lax.axis_size("chip")
    energies = 2 * chips
    width = green_less.shape[3]
    rows = width // energies
    half_shape = (chips, 2, rows, width)
    full_shape = (energies, 2, rows, width)

    def swap_cores(value):
        return lax.ppermute(value, "core", [(0, 1), (1, 0)])

    def to_partner(keep, got):
        routes = run_kernel(
            sort_body, [((2, 2, rows, width), BF16)] * chips, (keep, got)
        )
        sent = []
        for step, route in enumerate(routes):
            pairs = [
                (chip * 2 + side, (chip ^ step) * 2 + 1 - side)
                for chip in range(chips)
                for side in range(2)
            ]
            sent.append(lax.ppermute(route, ("chip", "half"), pairs))
        return sent

    def regroup(value):
        return lax.all_to_all(value, ("chip", "core"), split_axis=0, concat_axis=0, tiled=True)

    away, keep = run_kernel(
        split_body,
        [(half_shape, BF16)] * 2,
        (green_greater.reshape(2, chips, 2, rows, width),),
    )
    more = to_partner(keep, swap_cores(away))
    (turned,) = run_kernel(turn_body, [(full_shape, BF16)], (green_less,))
    less = regroup(turned)
    own, away, keep = run_kernel(
        lag_body,
        [(full_shape, BF16), (half_shape, BF16), (half_shape, BF16)],
        (less, *more),
        scratch=[pltpu.VMEM(full_shape, BF16)],
        flops=energies * (energies + 1) * 4 * rows * width,
    )
    other = to_partner(keep, swap_cores(away))
    term, coupling, weight = run_kernel(
        own_body,
        [((2, width, width), F32), ((width, width), BF16), ((8, 128), F32)],
        (
            pair_blocks,
            onsite_scale,
            coupling_scale,
            coupling_mask,
            regroup(own),
            onsite_block,
            coupling_block,
        ),
        specs=[SMEM] * 4 + [VMEM] * 3,
        flops=8 * width**3,
    )
    (screened,) = run_kernel(
        join_body,
        [((2, 1, width, width), BF16)],
        (*other, term, coupling, weight),
        scratch=[pltpu.VMEM((2, width, width), BF16)],
        flops=8 * width**3,
    )
    return screened


def solution(mesh):
    energies, pairs = mesh.shape["energy"], mesh.shape["pair"]
    fine = Mesh(
        mesh.devices.reshape(energies // 2, 2, 2, pairs // 2), ("chip", "core", "half", "low")
    )
    across_mesh = P(None, ("chip", "core"), ("half", "low"), None)
    return jax.shard_map(
        on_device,
        mesh=fine,
        in_specs=(across_mesh, across_mesh, P(("half", "low"), None), P(), P(), P(), P(), P()),
        out_specs=across_mesh,
        check_vma=False,
    )
```

```python
import functools

import jax
import jax.numpy as jnp
from jax import lax
from jax.experimental import pallas as pl
from jax.experimental.pallas import tpu as pltpu
from jax.sharding import Mesh
from jax.sharding import PartitionSpec as P

BF16 = jnp.bfloat16
F32 = jnp.float32
VMEM = pl.BlockSpec(memory_space=pltpu.VMEM)
SMEM = pl.BlockSpec(memory_space=pltpu.SMEM)


def run_kernel(body, outs, args, specs=None, scratch=(), flops=0):
    return pl.pallas_call(
        body,
        out_shape=[jax.ShapeDtypeStruct(shape, dtype) for shape, dtype in outs],
        in_specs=specs or [VMEM] * len(args),
        out_specs=[VMEM] * len(outs),
        scratch_shapes=list(scratch),
        compiler_params=pltpu.CompilerParams(vmem_limit_bytes=12 * 2**20),
        cost_estimate=pl.CostEstimate(flops=flops, bytes_accessed=2**19, transcendentals=0),
    )(*args)


def pack_body(less, more, packed):
    half = lax.axis_index("half")
    groups, _, _, rows, _ = packed.shape
    for part in range(2):
        flipped = less[part, 0].astype(F32).T.astype(BF16)
        for group in range(groups):
            span = slice(group * rows, (group + 1) * rows)
            packed[group, half, part] = flipped[span]
            packed[group, 1 - half, part] = more[part, 0, span]


def lag_body(given, polar):
    half = lax.axis_index("half")
    energies, _, _, rows, width = given.shape
    factor = energies ** (-0.5)
    for top in range(0, rows, 16):
        for left in range(0, width, 128):
            at = (pl.ds(top, 16), pl.ds(left, 128))
            for lag in range(energies):
                real = jnp.zeros((16, 128), F32)
                imag = jnp.zeros((16, 128), F32)
                for late in range(lag, energies):
                    lr = given[(late, half, 0) + at].astype(F32)
                    li = given[(late, half, 1) + at].astype(F32)
                    mr = given[(late - lag, 1 - half, 0) + at].astype(F32)
                    mi = given[(late - lag, 1 - half, 1) + at].astype(F32)
                    real += lr * mr - li * mi
                    imag += lr * mi + li * mr
                for side in range(2):
                    polar[(lag, side, 0) + at] = (factor * imag).astype(BF16)
                    polar[(lag, side, 1) + at] = (-factor * real).astype(BF16)


def across(left, turned):
    return lax.dot_general(
        left, turned, (((1,), (1,)), ((), ())), preferred_element_type=F32
    ).astype(BF16)


def screen_body(blocks, onsite_scale, coupling_scale, mask, polar, onsite, link, out, coupling):
    half = lax.axis_index("half")
    width = onsite.shape[0]
    row, col = blocks[0, 0], blocks[0, 1]
    low = jnp.minimum(row, col)
    scale = onsite_scale[row] * onsite_scale[col]
    strength = coupling_scale[low]
    weight = mask[low, low + 1].astype(F32) * strength * strength

    @pl.when(row < col)
    def _():
        coupling[...] = link[...]

    @pl.when(row >= col)
    def _():
        coupling[...] = link[...].astype(F32).T.astype(BF16)

    for part in range(2):
        own = polar[:, half, part].reshape(width, width)
        other = polar[:, 1 - half, part].reshape(width, width)
        inner = across(onsite[...], own)
        term = scale * jnp.dot(inner, onsite[...], preferred_element_type=F32)
        inner = across(coupling[...], other)
        mirrored = weight * jnp.dot(inner, coupling[...], preferred_element_type=F32)
        out[part, 0] = (term + mirrored.astype(BF16).astype(F32)).astype(BF16)


def on_device(
    green_less,
    green_greater,
    pair_blocks,
    onsite_scale,
    coupling_scale,
    coupling_mask,
    onsite_block,
    coupling_block,
):
    energies = 2 * lax.axis_size("chip")
    width = green_less.shape[3]
    rows = width // energies
    shape = (energies, 2, 2, rows, width)

    def regroup(value):
        flat = value.reshape((2 * energies,) + shape[2:])
        axes = ("chip", "core", "half")
        return lax.all_to_all(flat, axes, split_axis=0, concat_axis=0, tiled=True).reshape(shape)

    (packed,) = run_kernel(pack_body, [(shape, BF16)], (green_less, green_greater))
    (polar,) = run_kernel(
        lag_body,
        [(shape, BF16)],
        (regroup(packed),),
        flops=energies * (energies + 1) * 4 * rows * width,
    )
    (screened,) = run_kernel(
        screen_body,
        [((2, 1, width, width), BF16)],
        (
            pair_blocks,
            onsite_scale,
            coupling_scale,
            coupling_mask,
            regroup(polar),
            onsite_block,
            coupling_block,
        ),
        specs=[SMEM] * 4 + [VMEM] * 3,
        scratch=[pltpu.VMEM((width, width), BF16)],
        flops=16 * width**3,
    )
    return screened


def solution(mesh):
    energies, pairs = mesh.shape["energy"], mesh.shape["pair"]
    fine = Mesh(
        mesh.devices.reshape(energies // 2, 2, 2, pairs // 2), ("chip", "core", "half", "low")
    )
    across_mesh = P(None, ("chip", "core"), ("half", "low"), None)
    return jax.shard_map(
        on_device,
        mesh=fine,
        in_specs=(across_mesh, across_mesh, P(("half", "low"), None), P(), P(), P(), P(), P()),
        out_specs=across_mesh,
        check_vma=False,
    )
```

```python
import functools

import jax
import jax.numpy as jnp
from jax import lax
from jax.experimental import pallas as pl
from jax.experimental.pallas import tpu as pltpu
from jax.sharding import Mesh
from jax.sharding import PartitionSpec as P

BF16 = jnp.bfloat16
F32 = jnp.float32
VMEM = pl.BlockSpec(memory_space=pltpu.VMEM)
SMEM = pl.BlockSpec(memory_space=pltpu.SMEM)
HBM = pl.BlockSpec(memory_space=pltpu.HBM)


def run_kernel(body, outs, args, specs=None, out_specs=None, scratch=(), flops=0):
    return pl.pallas_call(
        body,
        out_shape=[jax.ShapeDtypeStruct(shape, dtype) for shape, dtype in outs],
        in_specs=specs or [VMEM] * len(args),
        out_specs=out_specs or [VMEM] * len(outs),
        scratch_shapes=list(scratch),
        compiler_params=pltpu.CompilerParams(vmem_limit_bytes=12 * 2**20),
        cost_estimate=pl.CostEstimate(flops=flops, bytes_accessed=2**19, transcendentals=0),
    )(*args)


def rows_of(first, rows):
    return pl.ds(pl.multiple_of(first * rows, rows), rows)


def order_of(chips, second):
    plane = [(0, step) for step in range(1, chips)]
    cross = [(1, step) for step in range(chips)]
    return plane + cross if second else cross + plane


def in_second():
    return 2 * lax.axis_index("low") >= lax.axis_size("low")


def turn_of(chips, turn):
    second = in_second()
    return [
        jnp.where(second, late, soon)
        for soon, late in zip(order_of(chips, False)[turn], order_of(chips, True)[turn])
    ]


def pack_body(less, more, away, keep, held, turned, sems):
    chip, core = lax.axis_index("chip"), lax.axis_index("core")
    copies = [
        pltpu.make_async_copy(source, held.at[place], sems.at[place])
        for place, source in enumerate((less, more))
    ]
    for copy in copies:
        copy.start()
    rows = away.shape[3]
    for kind in range(2):
        copies[kind].wait()
        for part in range(2):
            whole = held[kind, part, 0]
            if kind == 0:
                whole = whole.astype(F32).T.astype(BF16)
            turned[part] = whole
        for place in range(away.shape[0]):
            first = 2 * (chip ^ place)
            away[place, kind] = turned[:, rows_of(first + 1 - core, rows)]
            keep[place, kind] = turned[:, rows_of(first + core, rows)]


def pair_body(keep, got, *blocks):
    chips, kinds = keep.shape[:2]
    for turn, block in enumerate(blocks):
        crosses, step = turn_of(chips, turn)
        kind = crosses if kinds == 2 else 0
        block[0] = keep[step, kind]
        block[1] = got[step, kind]


def lag_body(keep, got, *refs):
    blocks, (away, kept, joined, polar) = refs[:-4], refs[-4:]
    chip, core = lax.axis_index("chip"), lax.axis_index("core")
    energies, _, rows, width = polar.shape
    chips = energies // 2
    joined[2 * chip + core, 0] = keep[0, 0]
    joined[2 * chip + 1 - core, 0] = got[0, 0]
    for turn, block in enumerate(blocks):
        crosses, step = turn_of(chips, turn)
        joined[2 * (chip ^ step) + core, crosses] = block[0]
        joined[2 * (chip ^ step) + 1 - core, crosses] = block[1]
    factor = energies ** (-0.5)
    for top in range(0, rows, 16):
        for left in range(0, width, 128):
            at = (pl.ds(top, 16), pl.ds(left, 128))
            for lag in range(energies):
                real = imag = jnp.zeros((16, 128), F32)
                for late in range(lag, energies):
                    lr = joined[(late, 0, 0) + at].astype(F32)
                    li = joined[(late, 0, 1) + at].astype(F32)
                    mr = joined[(late - lag, 1, 0) + at].astype(F32)
                    mi = joined[(late - lag, 1, 1) + at].astype(F32)
                    real += lr * mr - li * mi
                    imag += lr * mi + li * mr
                polar[(lag, 0) + at] = (factor * imag).astype(BF16)
                polar[(lag, 1) + at] = (-factor * real).astype(BF16)
    for place in range(chips):
        first = 2 * (chip ^ place)
        away[place, 0] = polar[first + 1 - core]
        kept[place, 0] = polar[first + core]


def across(left, turned):
    return lax.dot_general(
        left, turned, (((1,), (1,)), ((), ())), preferred_element_type=F32
    ).astype(BF16)


def weigh_body(blocks, onsite_scale, coupling_scale, mask, link, _, coupling, weights):
    row, col = blocks[0, 0], blocks[0, 1]
    low = jnp.minimum(row, col)
    strength = coupling_scale[low]
    weights[0] = jnp.full(weights.shape[1:], onsite_scale[row] * onsite_scale[col], F32)
    weights[1] = jnp.full(
        weights.shape[1:], mask[low, low + 1].astype(F32) * strength * strength, F32
    )

    @pl.when(row < col)
    def _():
        coupling[...] = link[...]

    @pl.when(row >= col)
    def _():
        coupling[...] = link[...].astype(F32).T.astype(BF16)


def screen_body(onsite, coupling, weights, keep, got, *refs):
    blocks = refs[:-4]
    out, whole, ready, sems = refs[-4:]
    chip, core = lax.axis_index("chip"), lax.axis_index("core")
    chips, _, _, rows, _ = keep.shape

    def put(slot, step, mine, theirs):
        whole[slot, :, rows_of(2 * (chip ^ step) + core, rows)] = mine
        whole[slot, :, rows_of(2 * (chip ^ step) + 1 - core, rows)] = theirs

    put(0, 0, keep[0, 0], got[0, 0])
    for turn, block in enumerate(blocks):
        crosses, step = turn_of(chips, turn)
        put(crosses, step, block[0], block[1])
    copies = []
    for part in range(2):
        inner = across(onsite[...], whole[0, part])
        term = weights[0, 0, 0] * jnp.dot(inner, onsite[...], preferred_element_type=F32)
        inner = across(coupling[...], whole[1, part])
        mirrored = weights[1, 0, 0] * jnp.dot(inner, coupling[...], preferred_element_type=F32)
        ready[part, 0] = (term + mirrored.astype(BF16).astype(F32)).astype(BF16)
        copies.append(pltpu.make_async_copy(ready.at[part], out.at[part], sems.at[part]))
        copies[-1].start()
    for copy in copies:
        copy.wait()


def on_device(
    green_less,
    green_greater,
    pair_blocks,
    onsite_scale,
    coupling_scale,
    coupling_mask,
    onsite_block,
    coupling_block,
):
    chips, lows = lax.axis_size("chip"), lax.axis_size("low")
    energies = 2 * chips
    width = green_less.shape[3]
    rows = width // energies

    def piles(kinds):
        return ((chips, kinds, 2, rows, width), BF16)

    def spread(away, keep):
        got = lax.ppermute(away, "core", [(0, 1), (1, 0)])
        turns = 2 * chips - 1
        blocks = run_kernel(pair_body, [((2, 2, rows, width), BF16)] * turns, (keep, got))
        came = []
        for turn, block in enumerate(blocks):
            pairs = []
            for chip in range(chips):
                for half in range(2):
                    for low in range(lows):
                        crosses, step = order_of(chips, 2 * low >= lows)[turn]
                        source = (chip * 2 + half) * lows + low
                        target = ((chip ^ step) * 2 + (half ^ crosses)) * lows + low
                        pairs.append((source, target))
            came.append(lax.ppermute(block, ("chip", "half", "low"), pairs))
        return keep, got, *came

    away, keep = run_kernel(
        pack_body,
        [piles(2)] * 2,
        (green_less, green_greater),
        specs=[HBM] * 2,
        scratch=[
            pltpu.VMEM((2, 2, 1, width, width), BF16),
            pltpu.VMEM((2, width, width), BF16),
            pltpu.SemaphoreType.DMA((2,)),
        ],
    )
    away, keep = run_kernel(
        lag_body,
        [piles(1)] * 2,
        spread(away, keep),
        scratch=[
            pltpu.VMEM((energies, 2, 2, rows, width), BF16),
            pltpu.VMEM((energies, 2, rows, width), BF16),
        ],
        flops=energies * (energies + 1) * 4 * rows * width,
    )
    parts = spread(away, keep)
    coupling, weights = run_kernel(
        weigh_body,
        [((width, width), BF16), ((2, 8, 128), F32)],
        (pair_blocks, onsite_scale, coupling_scale, coupling_mask, coupling_block, away),
        specs=[SMEM] * 4 + [VMEM] * 2,
    )
    (screened,) = run_kernel(
        screen_body,
        [((2, 1, width, width), BF16)],
        (onsite_block, coupling, weights, *parts),
        out_specs=[HBM],
        scratch=[
            pltpu.VMEM((2, 2, width, width), BF16),
            pltpu.VMEM((2, 1, width, width), BF16),
            pltpu.SemaphoreType.DMA((2,)),
        ],
        flops=16 * width**3,
    )
    return screened


def solution(mesh):
    energies, pairs = mesh.shape["energy"], mesh.shape["pair"]
    fine = Mesh(
        mesh.devices.reshape(energies // 2, 2, 2, pairs // 2), ("chip", "core", "half", "low")
    )
    across_mesh = P(None, ("chip", "core"), ("half", "low"), None)
    return jax.shard_map(
        on_device,
        mesh=fine,
        in_specs=(across_mesh, across_mesh, P(("half", "low"), None), P(), P(), P(), P(), P()),
        out_specs=across_mesh,
        check_vma=False,
    )
```

```python
import functools

import jax
import jax.numpy as jnp
from jax import lax
from jax.experimental import pallas as pl
from jax.experimental.pallas import tpu as pltpu
from jax.sharding import Mesh
from jax.sharding import PartitionSpec as P

BF16 = jnp.bfloat16
F32 = jnp.float32
VMEM = pl.BlockSpec(memory_space=pltpu.VMEM)
SMEM = pl.BlockSpec(memory_space=pltpu.SMEM)
HBM = pl.BlockSpec(memory_space=pltpu.HBM)


def run_kernel(body, outs, args, specs=None, out_specs=None, scratch=(), flops=0):
    return pl.pallas_call(
        body,
        out_shape=[jax.ShapeDtypeStruct(shape, dtype) for shape, dtype in outs],
        in_specs=specs or [VMEM] * len(args),
        out_specs=out_specs or [VMEM] * len(outs),
        scratch_shapes=list(scratch),
        compiler_params=pltpu.CompilerParams(vmem_limit_bytes=12 * 2**20),
        cost_estimate=pl.CostEstimate(flops=flops, bytes_accessed=2**19, transcendentals=0),
    )(*args)


def rows_of(first, rows):
    return pl.ds(pl.multiple_of(first * rows, rows), rows)


def order_of(chips, second):
    plane = [(0, step) for step in reversed(range(1, chips))]
    cross = [(1, step) for step in range(chips)]
    return plane + cross if second else cross + plane


def in_second():
    return 2 * lax.axis_index("low") >= lax.axis_size("low")


def turn_of(chips, turn):
    second = in_second()
    return [
        jnp.where(second, late, soon)
        for soon, late in zip(order_of(chips, False)[turn], order_of(chips, True)[turn])
    ]


def pack_body(less, more, first, away, keep, held, turned, sems):
    chip, core = lax.axis_index("chip"), lax.axis_index("core")
    copies = [
        pltpu.make_async_copy(source, held.at[place], sems.at[place])
        for place, source in enumerate((less, more))
    ]
    for copy in copies:
        copy.start()
    chips, _, _, rows, _ = away.shape
    for kind in range(2):
        copies[kind].wait()
        for part in range(2):
            whole = held[kind, part, 0]
            if kind == 0:
                whole = whole.astype(F32).T.astype(BF16)
            turned[kind, part] = whole
    crosses, step = turn_of(chips, 0)
    for owner in range(2):
        first[owner] = turned[crosses, :, rows_of(2 * (chip ^ step) + owner, rows)]
    for kind in range(2):
        for place in range(chips):
            top = 2 * (chip ^ place)
            away[place, kind] = turned[kind, :, rows_of(top + 1 - core, rows)]
            keep[place, kind] = turned[kind, :, rows_of(top + core, rows)]


def pair_body(keep, got, *blocks):
    chips, kinds = keep.shape[:2]
    for turn, block in enumerate(blocks, 1):
        crosses, step = turn_of(chips, turn)
        kind = crosses if kinds == 2 else 0
        block[0] = keep[step, kind]
        block[1] = got[step, kind]


def late_body(came, _, away):
    away[...] = came[1 - lax.axis_index("core")]


def sort_blocks(chips, blocks, late, put):
    core = lax.axis_index("core")
    for turn, block in enumerate(blocks):
        crosses, step = turn_of(chips, turn)
        if turn == 0:
            put(crosses, step, block[core], late[...])
        else:
            put(crosses, step, block[0], block[1])


def lag_body(keep, got, late, *refs):
    blocks, (first, away, kept, joined, polar) = refs[:-5], refs[-5:]
    chip, core = lax.axis_index("chip"), lax.axis_index("core")
    energies, _, rows, width = polar.shape
    chips = energies // 2

    def put(crosses, step, mine, theirs):
        joined[2 * (chip ^ step) + core, crosses] = mine
        joined[2 * (chip ^ step) + 1 - core, crosses] = theirs

    put(0, 0, keep[0, 0], got[0, 0])
    sort_blocks(chips, blocks, late, put)
    factor = energies ** (-0.5)
    for top in range(0, rows, 16):
        for left in range(0, width, 128):
            at = (pl.ds(top, 16), pl.ds(left, 128))
            for lag in range(energies):
                real = imag = jnp.zeros((16, 128), F32)
                for late in range(lag, energies):
                    lr = joined[(late, 0, 0) + at].astype(F32)
                    li = joined[(late, 0, 1) + at].astype(F32)
                    mr = joined[(late - lag, 1, 0) + at].astype(F32)
                    mi = joined[(late - lag, 1, 1) + at].astype(F32)
                    real += lr * mr - li * mi
                    imag += lr * mi + li * mr
                polar[(lag, 0) + at] = (factor * imag).astype(BF16)
                polar[(lag, 1) + at] = (-factor * real).astype(BF16)
    _, step = turn_of(chips, 0)
    for owner in range(2):
        first[owner] = polar[2 * (chip ^ step) + owner]
    for place in range(chips):
        top = 2 * (chip ^ place)
        away[place, 0] = polar[top + 1 - core]
        kept[place, 0] = polar[top + core]


def across(left, turned):
    return lax.dot_general(
        left, turned, (((1,), (1,)), ((), ())), preferred_element_type=F32
    ).astype(BF16)


def weigh_body(blocks, onsite_scale, coupling_scale, mask, link, _, coupling, weights):
    row, col = blocks[0, 0], blocks[0, 1]
    low = jnp.minimum(row, col)
    strength = coupling_scale[low]
    weights[0] = jnp.full(weights.shape[1:], onsite_scale[row] * onsite_scale[col], F32)
    weights[1] = jnp.full(
        weights.shape[1:], mask[low, low + 1].astype(F32) * strength * strength, F32
    )

    @pl.when(row < col)
    def _():
        coupling[...] = link[...]

    @pl.when(row >= col)
    def _():
        coupling[...] = link[...].astype(F32).T.astype(BF16)


def screen_body(onsite, coupling, weights, keep, got, late, *refs):
    blocks = refs[:-4]
    out, whole, ready, sems = refs[-4:]
    chip, core = lax.axis_index("chip"), lax.axis_index("core")
    chips, _, _, rows, _ = keep.shape

    def put(slot, step, mine, theirs):
        whole[slot, :, rows_of(2 * (chip ^ step) + core, rows)] = mine
        whole[slot, :, rows_of(2 * (chip ^ step) + 1 - core, rows)] = theirs

    put(0, 0, keep[0, 0], got[0, 0])
    sort_blocks(chips, blocks, late, put)
    copies = []
    for part in range(2):
        inner = across(onsite[...], whole[0, part])
        term = weights[0, 0, 0] * jnp.dot(inner, onsite[...], preferred_element_type=F32)
        inner = across(coupling[...], whole[1, part])
        mirrored = weights[1, 0, 0] * jnp.dot(inner, coupling[...], preferred_element_type=F32)
        ready[part, 0] = (term + mirrored.astype(BF16).astype(F32)).astype(BF16)
        copies.append(pltpu.make_async_copy(ready.at[part], out.at[part], sems.at[part]))
        copies[-1].start()
    for copy in copies:
        copy.wait()


def on_device(
    green_less,
    green_greater,
    pair_blocks,
    onsite_scale,
    coupling_scale,
    coupling_mask,
    onsite_block,
    coupling_block,
):
    chips, lows = lax.axis_size("chip"), lax.axis_size("low")
    energies = 2 * chips
    width = green_less.shape[3]
    rows = width // energies

    def piles(kinds):
        return ((chips, kinds, 2, rows, width), BF16)

    block_shape = ((2, 2, rows, width), BF16)

    def swap_cores(value):
        return lax.ppermute(value, "core", [(0, 1), (1, 0)])

    def spread(first, away, keep):
        got = swap_cores(away)
        later = run_kernel(pair_body, [block_shape] * (2 * chips - 2), (keep, got))
        came = []
        for turn, block in enumerate((first, *later)):
            pairs = []
            for chip in range(chips):
                for half in range(2):
                    for low in range(lows):
                        crosses, step = order_of(chips, 2 * low >= lows)[turn]
                        source = (chip * 2 + half) * lows + low
                        target = ((chip ^ step) * 2 + (half ^ crosses)) * lows + low
                        pairs.append((source, target))
            came.append(lax.ppermute(block, ("chip", "half", "low"), pairs))
        (away,) = run_kernel(late_body, [((2, rows, width), BF16)], (came[0], came[1]))
        return keep, got, swap_cores(away), *came

    first, away, keep = run_kernel(
        pack_body,
        [block_shape] + [piles(2)] * 2,
        [pltpu.with_memory_space_constraint(value, pltpu.HBM) for value in (green_less, green_greater)],
        specs=[HBM] * 2,
        scratch=[
            pltpu.VMEM((2, 2, 1, width, width), BF16),
            pltpu.VMEM((2, 2, width, width), BF16),
            pltpu.SemaphoreType.DMA((2,)),
        ],
    )
    first, away, keep = run_kernel(
        lag_body,
        [block_shape] + [piles(1)] * 2,
        spread(first, away, keep),
        scratch=[
            pltpu.VMEM((energies, 2, 2, rows, width), BF16),
            pltpu.VMEM((energies, 2, rows, width), BF16),
        ],
        flops=energies * (energies + 1) * 4 * rows * width,
    )
    parts = spread(first, away, keep)
    coupling, weights = run_kernel(
        weigh_body,
        [((width, width), BF16), ((2, 8, 128), F32)],
        (pair_blocks, onsite_scale, coupling_scale, coupling_mask, coupling_block, away),
        specs=[SMEM] * 4 + [VMEM] * 2,
    )
    (screened,) = run_kernel(
        screen_body,
        [((2, 1, width, width), BF16)],
        (onsite_block, coupling, weights, *parts),
        out_specs=[HBM],
        scratch=[
            pltpu.VMEM((2, 2, width, width), BF16),
            pltpu.VMEM((2, 1, width, width), BF16),
            pltpu.SemaphoreType.DMA((2,)),
        ],
        flops=16 * width**3,
    )
    return screened


def solution(mesh):
    energies, pairs = mesh.shape["energy"], mesh.shape["pair"]
    fine = Mesh(
        mesh.devices.reshape(energies // 2, 2, 2, pairs // 2), ("chip", "core", "half", "low")
    )
    across_mesh = P(None, ("chip", "core"), ("half", "low"), None)
    return jax.shard_map(
        on_device,
        mesh=fine,
        in_specs=(across_mesh, across_mesh, P(("half", "low"), None), P(), P(), P(), P(), P()),
        out_specs=across_mesh,
        check_vma=False,
    )
```

```python
import functools

import jax
import jax.numpy as jnp
from jax import lax
from jax.experimental import pallas as pl
from jax.experimental.pallas import tpu as pltpu
from jax.sharding import Mesh
from jax.sharding import PartitionSpec as P

BF16 = jnp.bfloat16
F32 = jnp.float32
VMEM = pl.BlockSpec(memory_space=pltpu.VMEM)
SMEM = pl.BlockSpec(memory_space=pltpu.SMEM)
HBM = pl.BlockSpec(memory_space=pltpu.HBM)


def run_kernel(body, outs, args, specs=None, out_specs=None, scratch=(), flops=0):
    return pl.pallas_call(
        body,
        out_shape=[jax.ShapeDtypeStruct(shape, dtype) for shape, dtype in outs],
        in_specs=specs or [VMEM] * len(args),
        out_specs=out_specs or [VMEM] * len(outs),
        scratch_shapes=list(scratch),
        compiler_params=pltpu.CompilerParams(vmem_limit_bytes=12 * 2**20),
        cost_estimate=pl.CostEstimate(flops=flops, bytes_accessed=2**19, transcendentals=0),
    )(*args)


def rows_of(first, rows):
    return pl.ds(pl.multiple_of(first * rows, rows), rows)


def order_of(chips, second, phase):
    plane = [(0, step) for step in reversed(range(1, chips))]
    cross = [(1, step) for step in range(chips)]
    if second:
        return plane[:-1] + cross[:1] + plane[-1:] + cross[1:]
    return cross + plane


def in_second():
    return 2 * lax.axis_index("low") >= lax.axis_size("low")


def turn_of(chips, turn, phase):
    second = in_second()
    return [
        jnp.where(second, late, soon)
        for soon, late in zip(order_of(chips, False, phase)[turn], order_of(chips, True, phase)[turn])
    ]


def pack_body(less, more, first, away, keep, held, turned, sems):
    chip, core = lax.axis_index("chip"), lax.axis_index("core")
    copies = [
        pltpu.make_async_copy(source, held.at[place], sems.at[place])
        for place, source in enumerate((less, more))
    ]
    for copy in copies:
        copy.start()
    chips, _, _, rows, _ = away.shape
    for kind in range(2):
        copies[kind].wait()
        for part in range(2):
            whole = held[kind, part, 0]
            if kind == 0:
                whole = whole.astype(F32).T.astype(BF16)
            turned[kind, part] = whole
    crosses, step = turn_of(chips, 0, 0)
    for owner in range(2):
        first[owner] = turned[crosses, :, rows_of(2 * (chip ^ step) + owner, rows)]
    for kind in range(2):
        for place in range(chips):
            top = 2 * (chip ^ place)
            away[place, kind] = turned[kind, :, rows_of(top + 1 - core, rows)]
            keep[place, kind] = turned[kind, :, rows_of(top + core, rows)]


def pair_body(phase, keep, got, *blocks):
    chips, kinds = keep.shape[:2]
    for turn, block in enumerate(blocks, 1):
        crosses, step = turn_of(chips, turn, phase)
        kind = crosses if kinds == 2 else 0
        block[0] = keep[step, kind]
        block[1] = got[step, kind]


def late_body(came, _, away):
    away[...] = came[1 - lax.axis_index("core")]


def sort_blocks(chips, phase, blocks, late, put):
    core = lax.axis_index("core")
    for turn, block in enumerate(blocks):
        crosses, step = turn_of(chips, turn, phase)
        if turn == 0:
            put(crosses, step, block[core], late[...])
        else:
            put(crosses, step, block[0], block[1])


def lag_body(keep, got, late, *refs):
    blocks, (first, away, kept, joined, polar) = refs[:-5], refs[-5:]
    chip, core = lax.axis_index("chip"), lax.axis_index("core")
    energies, _, rows, width = polar.shape
    chips = energies // 2

    def put(crosses, step, mine, theirs):
        joined[2 * (chip ^ step) + core, crosses] = mine
        joined[2 * (chip ^ step) + 1 - core, crosses] = theirs

    put(0, 0, keep[0, 0], got[0, 0])
    sort_blocks(chips, 0, blocks, late, put)
    factor = energies ** (-0.5)
    for top in range(0, rows, 16):
        for left in range(0, width, 128):
            at = (pl.ds(top, 16), pl.ds(left, 128))
            for lag in range(energies):
                real = imag = jnp.zeros((16, 128), F32)
                for late in range(lag, energies):
                    lr = joined[(late, 0, 0) + at].astype(F32)
                    li = joined[(late, 0, 1) + at].astype(F32)
                    mr = joined[(late - lag, 1, 0) + at].astype(F32)
                    mi = joined[(late - lag, 1, 1) + at].astype(F32)
                    real += lr * mr - li * mi
                    imag += lr * mi + li * mr
                polar[(lag, 0) + at] = (factor * imag).astype(BF16)
                polar[(lag, 1) + at] = (-factor * real).astype(BF16)
    _, step = turn_of(chips, 0, 1)
    for owner in range(2):
        first[owner] = polar[2 * (chip ^ step) + owner]
    for place in range(chips):
        top = 2 * (chip ^ place)
        away[place, 0] = polar[top + 1 - core]
        kept[place, 0] = polar[top + core]


def across(left, turned):
    return lax.dot_general(
        left, turned, (((1,), (1,)), ((), ())), preferred_element_type=F32
    ).astype(BF16)


def weigh_body(blocks, onsite_scale, coupling_scale, mask, link, _, coupling, weights):
    row, col = blocks[0, 0], blocks[0, 1]
    low = jnp.minimum(row, col)
    strength = coupling_scale[low]
    weights[0] = jnp.full(weights.shape[1:], onsite_scale[row] * onsite_scale[col], F32)
    weights[1] = jnp.full(
        weights.shape[1:], mask[low, low + 1].astype(F32) * strength * strength, F32
    )

    @pl.when(row < col)
    def _():
        coupling[...] = link[...]

    @pl.when(row >= col)
    def _():
        coupling[...] = link[...].astype(F32).T.astype(BF16)


def screen_body(onsite, coupling, weights, keep, got, late, *refs):
    blocks = refs[:-4]
    out, whole, ready, sems = refs[-4:]
    chip, core = lax.axis_index("chip"), lax.axis_index("core")
    chips, _, _, rows, width = keep.shape

    def put(slot, step, mine, theirs):
        whole[slot, :, rows_of(2 * (chip ^ step) + core, rows)] = mine
        whole[slot, :, rows_of(2 * (chip ^ step) + 1 - core, rows)] = theirs

    put(0, 0, keep[0, 0], got[0, 0])
    sort_blocks(chips, 1, blocks, late, put)
    copies = []
    inner_own = across(onsite[...], whole[0].reshape(2 * width, width))
    inner_other = across(coupling[...], whole[1].reshape(2 * width, width))
    for part in range(2):
        at = slice(part * width, (part + 1) * width)
        term = weights[0, 0, 0] * jnp.dot(
            inner_own[:, at], onsite[...], preferred_element_type=F32
        )
        mirrored = weights[1, 0, 0] * jnp.dot(
            inner_other[:, at], coupling[...], preferred_element_type=F32
        )
        ready[part, 0] = (term + mirrored.astype(BF16).astype(F32)).astype(BF16)
        copies.append(pltpu.make_async_copy(ready.at[part], out.at[part], sems.at[part]))
        copies[-1].start()
    for copy in copies:
        copy.wait()


def on_device(
    green_less,
    green_greater,
    pair_blocks,
    onsite_scale,
    coupling_scale,
    coupling_mask,
    onsite_block,
    coupling_block,
):
    chips, lows = lax.axis_size("chip"), lax.axis_size("low")
    energies = 2 * chips
    width = green_less.shape[3]
    rows = width // energies

    def piles(kinds):
        return ((chips, kinds, 2, rows, width), BF16)

    block_shape = ((2, 2, rows, width), BF16)

    def swap_cores(value):
        return lax.ppermute(value, "core", [(0, 1), (1, 0)])

    def spread(first, away, keep, phase):
        got = swap_cores(away)
        later = run_kernel(
            functools.partial(pair_body, phase), [block_shape] * (2 * chips - 2), (keep, got)
        )
        came = []
        for turn, block in enumerate((first, *later)):
            pairs = []
            for chip in range(chips):
                for half in range(2):
                    for low in range(lows):
                        crosses, step = order_of(chips, 2 * low >= lows, phase)[turn]
                        source = (chip * 2 + half) * lows + low
                        target = ((chip ^ step) * 2 + (half ^ crosses)) * lows + low
                        pairs.append((source, target))
            came.append(lax.ppermute(block, ("chip", "half", "low"), pairs))
        (away,) = run_kernel(late_body, [((2, rows, width), BF16)], (came[0], came[1]))
        return keep, got, swap_cores(away), *came

    first, away, keep = run_kernel(
        pack_body,
        [block_shape] + [piles(2)] * 2,
        [pltpu.with_memory_space_constraint(value, pltpu.HBM) for value in (green_less, green_greater)],
        specs=[HBM] * 2,
        scratch=[
            pltpu.VMEM((2, 2, 1, width, width), BF16),
            pltpu.VMEM((2, 2, width, width), BF16),
            pltpu.SemaphoreType.DMA((2,)),
        ],
    )
    first, away, keep = run_kernel(
        lag_body,
        [block_shape] + [piles(1)] * 2,
        spread(first, away, keep, 0),
        scratch=[
            pltpu.VMEM((energies, 2, 2, rows, width), BF16),
            pltpu.VMEM((energies, 2, rows, width), BF16),
        ],
        flops=energies * (energies + 1) * 4 * rows * width,
    )
    parts = spread(first, away, keep, 1)
    coupling, weights = run_kernel(
        weigh_body,
        [((width, width), BF16), ((2, 8, 128), F32)],
        (pair_blocks, onsite_scale, coupling_scale, coupling_mask, coupling_block, away),
        specs=[SMEM] * 4 + [VMEM] * 2,
    )
    (screened,) = run_kernel(
        screen_body,
        [((2, 1, width, width), BF16)],
        (onsite_block, coupling, weights, *parts),
        out_specs=[HBM],
        scratch=[
            pltpu.VMEM((2, 2, width, width), BF16),
            pltpu.VMEM((2, 1, width, width), BF16),
            pltpu.SemaphoreType.DMA((2,)),
        ],
        flops=16 * width**3,
    )
    return screened


def solution(mesh):
    energies, pairs = mesh.shape["energy"], mesh.shape["pair"]
    fine = Mesh(
        mesh.devices.reshape(energies // 2, 2, 2, pairs // 2), ("chip", "core", "half", "low")
    )
    across_mesh = P(None, ("chip", "core"), ("half", "low"), None)
    return jax.shard_map(
        on_device,
        mesh=fine,
        in_specs=(across_mesh, across_mesh, P(("half", "low"), None), P(), P(), P(), P(), P()),
        out_specs=across_mesh,
        check_vma=False,
    )
```

```python
import functools

import jax
import jax.numpy as jnp
from jax import lax
from jax.experimental import pallas as pl
from jax.experimental.pallas import tpu as pltpu
from jax.sharding import Mesh
from jax.sharding import PartitionSpec as P

BF16 = jnp.bfloat16
F32 = jnp.float32
VMEM = pl.BlockSpec(memory_space=pltpu.VMEM)
SMEM = pl.BlockSpec(memory_space=pltpu.SMEM)
HBM = pl.BlockSpec(memory_space=pltpu.HBM)
SOON = 2
TURNS = (
    ((0, 2, -3, 1, 3, -1, -2), (-3, -2, 3, 0, -1, 2, 1)),
    ((0, 1, -1, 3, -2, 2, -3), (-2, 0, 2, -3, -1, 1, 3)),
)


def run_kernel(body, outs, args, specs=None, out_specs=None, scratch=(), flops=0):
    return pl.pallas_call(
        body,
        out_shape=[jax.ShapeDtypeStruct(shape, dtype) for shape, dtype in outs],
        in_specs=specs or [VMEM] * len(args),
        out_specs=out_specs or [VMEM] * len(outs),
        scratch_shapes=list(scratch),
        compiler_params=pltpu.CompilerParams(vmem_limit_bytes=12 * 2**20),
        cost_estimate=pl.CostEstimate(flops=flops, bytes_accessed=2**19, transcendentals=0),
    )(*args)


def rows_of(first, rows):
    return pl.ds(pl.multiple_of(first * rows, rows), rows)


def order_of(chips, second, phase):
    if 2 * chips - 1 == len(TURNS[0][0]):
        turns = TURNS[phase][int(second)]
    else:
        cross, plane = list(range(chips)), [-step for step in reversed(range(1, chips))]
        turns = plane + cross if second else cross + plane
    return [(int(turn >= 0), abs(turn)) for turn in turns]


def in_second():
    return 2 * lax.axis_index("low") >= lax.axis_size("low")


def turn_of(chips, turn, phase):
    second = in_second()
    return [
        jnp.where(second, late, soon)
        for soon, late in zip(order_of(chips, False, phase)[turn], order_of(chips, True, phase)[turn])
    ]


def pack_body(less, more, *refs):
    soon, (away, keep, held, turned, sems) = refs[:SOON], refs[SOON:]
    chip, core = lax.axis_index("chip"), lax.axis_index("core")
    copies = [
        pltpu.make_async_copy(source, held.at[place], sems.at[place])
        for place, source in enumerate((less, more))
    ]
    for copy in copies:
        copy.start()
    chips, _, _, rows, _ = away.shape
    for kind in range(2):
        copies[kind].wait()
        for part in range(2):
            whole = held[kind, part, 0]
            if kind == 0:
                whole = whole.astype(F32).T.astype(BF16)
            turned[kind, part] = whole
    for turn, block in enumerate(soon):
        crosses, step = turn_of(chips, turn, 0)
        for owner in range(2):
            block[owner] = turned[crosses, :, rows_of(2 * (chip ^ step) + owner, rows)]
    for kind in range(2):
        for place in range(chips):
            top = 2 * (chip ^ place)
            away[place, kind] = turned[kind, :, rows_of(top + 1 - core, rows)]
            keep[place, kind] = turned[kind, :, rows_of(top + core, rows)]


def pair_body(phase, keep, got, *blocks):
    chips, kinds = keep.shape[:2]
    for turn, block in enumerate(blocks, SOON):
        crosses, step = turn_of(chips, turn, phase)
        kind = crosses if kinds == 2 else 0
        block[0] = keep[step, kind]
        block[1] = got[step, kind]


def late_body(*refs):
    away = refs[-1]
    for turn in range(SOON):
        away[turn] = refs[turn][1 - lax.axis_index("core")]


def sort_blocks(chips, phase, blocks, late, put):
    core = lax.axis_index("core")
    for turn, block in enumerate(blocks):
        crosses, step = turn_of(chips, turn, phase)
        if turn < SOON:
            put(crosses, step, block[core], late[turn])
        else:
            put(crosses, step, block[0], block[1])


def lag_body(keep, got, late, *refs):
    blocks, soon = refs[: -4 - SOON], refs[-4 - SOON : -4]
    away, kept, joined, polar = refs[-4:]
    chip, core = lax.axis_index("chip"), lax.axis_index("core")
    energies, _, rows, width = polar.shape
    chips = energies // 2

    def put(crosses, step, mine, theirs):
        joined[2 * (chip ^ step) + core, crosses] = mine
        joined[2 * (chip ^ step) + 1 - core, crosses] = theirs

    put(0, 0, keep[0, 0], got[0, 0])
    sort_blocks(chips, 0, blocks, late, put)
    factor = energies ** (-0.5)
    for top in range(0, rows, 16):
        for left in range(0, width, 128):
            at = (pl.ds(top, 16), pl.ds(left, 128))
            for lag in range(energies):
                real = imag = jnp.zeros((16, 128), F32)
                for late in range(lag, energies):
                    lr = joined[(late, 0, 0) + at].astype(F32)
                    li = joined[(late, 0, 1) + at].astype(F32)
                    mr = joined[(late - lag, 1, 0) + at].astype(F32)
                    mi = joined[(late - lag, 1, 1) + at].astype(F32)
                    real += lr * mr - li * mi
                    imag += lr * mi + li * mr
                polar[(lag, 0) + at] = (factor * imag).astype(BF16)
                polar[(lag, 1) + at] = (-factor * real).astype(BF16)
    for turn, block in enumerate(soon):
        _, step = turn_of(chips, turn, 1)
        for owner in range(2):
            block[owner] = polar[2 * (chip ^ step) + owner]
    for place in range(chips):
        top = 2 * (chip ^ place)
        away[place, 0] = polar[top + 1 - core]
        kept[place, 0] = polar[top + core]


def across(left, turned):
    return lax.dot_general(
        left, turned, (((1,), (1,)), ((), ())), preferred_element_type=F32
    ).astype(BF16)


def weigh_body(blocks, onsite_scale, coupling_scale, mask, link, _, coupling, weights):
    row, col = blocks[0, 0], blocks[0, 1]
    low = jnp.minimum(row, col)
    strength = coupling_scale[low]
    weights[0] = jnp.full(weights.shape[1:], onsite_scale[row] * onsite_scale[col], F32)
    weights[1] = jnp.full(
        weights.shape[1:], mask[low, low + 1].astype(F32) * strength * strength, F32
    )

    @pl.when(row < col)
    def _():
        coupling[...] = link[...]

    @pl.when(row >= col)
    def _():
        coupling[...] = link[...].astype(F32).T.astype(BF16)


def screen_body(onsite, coupling, weights, keep, got, late, *refs):
    blocks = refs[:-4]
    out, whole, ready, sems = refs[-4:]
    chip, core = lax.axis_index("chip"), lax.axis_index("core")
    chips, _, _, rows, width = keep.shape

    def put(slot, step, mine, theirs):
        whole[slot, :, rows_of(2 * (chip ^ step) + core, rows)] = mine
        whole[slot, :, rows_of(2 * (chip ^ step) + 1 - core, rows)] = theirs

    put(0, 0, keep[0, 0], got[0, 0])
    sort_blocks(chips, 1, blocks, late, put)
    copies = []
    inner_own = across(onsite[...], whole[0].reshape(2 * width, width))
    inner_other = across(coupling[...], whole[1].reshape(2 * width, width))
    for part in range(2):
        at = slice(part * width, (part + 1) * width)
        term = weights[0, 0, 0] * jnp.dot(
            inner_own[:, at], onsite[...], preferred_element_type=F32
        )
        mirrored = weights[1, 0, 0] * jnp.dot(
            inner_other[:, at], coupling[...], preferred_element_type=F32
        )
        ready[part, 0] = (term + mirrored.astype(BF16).astype(F32)).astype(BF16)
        copies.append(pltpu.make_async_copy(ready.at[part], out.at[part], sems.at[part]))
        copies[-1].start()
    for copy in copies:
        copy.wait()


def on_device(
    green_less,
    green_greater,
    pair_blocks,
    onsite_scale,
    coupling_scale,
    coupling_mask,
    onsite_block,
    coupling_block,
):
    chips, lows = lax.axis_size("chip"), lax.axis_size("low")
    energies = 2 * chips
    width = green_less.shape[3]
    rows = width // energies

    def piles(kinds):
        return ((chips, kinds, 2, rows, width), BF16)

    block_shape = ((2, 2, rows, width), BF16)

    def swap_cores(value):
        return lax.ppermute(value, "core", [(0, 1), (1, 0)])

    def spread(soon, away, keep, phase):
        got = swap_cores(away)
        later = run_kernel(
            functools.partial(pair_body, phase), [block_shape] * (2 * chips - 1 - SOON), (keep, got)
        )
        came = []
        for turn, block in enumerate((*soon, *later)):
            pairs = []
            for chip in range(chips):
                for half in range(2):
                    for low in range(lows):
                        crosses, step = order_of(chips, 2 * low >= lows, phase)[turn]
                        source = (chip * 2 + half) * lows + low
                        target = ((chip ^ step) * 2 + (half ^ crosses)) * lows + low
                        pairs.append((source, target))
            came.append(lax.ppermute(block, ("chip", "half", "low"), pairs))
        (away,) = run_kernel(late_body, [((SOON, 2, rows, width), BF16)], (*came[:SOON], later[0], came[3]))
        return keep, got, swap_cores(away), *came

    *soon, away, keep = run_kernel(
        pack_body,
        [block_shape] * SOON + [piles(2)] * 2,
        [pltpu.with_memory_space_constraint(value, pltpu.HBM) for value in (green_less, green_greater)],
        specs=[HBM] * 2,
        scratch=[
            pltpu.VMEM((2, 2, 1, width, width), BF16),
            pltpu.VMEM((2, 2, width, width), BF16),
            pltpu.SemaphoreType.DMA((2,)),
        ],
    )
    *soon, away, keep = run_kernel(
        lag_body,
        [block_shape] * SOON + [piles(1)] * 2,
        spread(soon, away, keep, 0),
        scratch=[
            pltpu.VMEM((energies, 2, 2, rows, width), BF16),
            pltpu.VMEM((energies, 2, rows, width), BF16),
        ],
        flops=energies * (energies + 1) * 4 * rows * width,
    )
    parts = spread(soon, away, keep, 1)
    coupling, weights = run_kernel(
        weigh_body,
        [((width, width), BF16), ((2, 8, 128), F32)],
        (pair_blocks, onsite_scale, coupling_scale, coupling_mask, coupling_block, away),
        specs=[SMEM] * 4 + [VMEM] * 2,
    )
    (screened,) = run_kernel(
        screen_body,
        [((2, 1, width, width), BF16)],
        (onsite_block, coupling, weights, *parts),
        out_specs=[HBM],
        scratch=[
            pltpu.VMEM((2, 2, width, width), BF16),
            pltpu.VMEM((2, 1, width, width), BF16),
            pltpu.SemaphoreType.DMA((2,)),
        ],
        flops=16 * width**3,
    )
    return screened


def solution(mesh):
    energies, pairs = mesh.shape["energy"], mesh.shape["pair"]
    fine = Mesh(
        mesh.devices.reshape(energies // 2, 2, 2, pairs // 2), ("chip", "core", "half", "low")
    )
    across_mesh = P(None, ("chip", "core"), ("half", "low"), None)
    return jax.shard_map(
        on_device,
        mesh=fine,
        in_specs=(across_mesh, across_mesh, P(("half", "low"), None), P(), P(), P(), P(), P()),
        out_specs=across_mesh,
        check_vma=False,
    )
```

```python
import functools

import jax
import jax.numpy as jnp
from jax import lax
from jax.experimental import pallas as pl
from jax.experimental.pallas import tpu as pltpu
from jax.sharding import Mesh
from jax.sharding import PartitionSpec as P

BF16 = jnp.bfloat16
F32 = jnp.float32
VMEM = pl.BlockSpec(memory_space=pltpu.VMEM)
SMEM = pl.BlockSpec(memory_space=pltpu.SMEM)
HBM = pl.BlockSpec(memory_space=pltpu.HBM)
SOON = 2
TURNS = (
    ((0, 2, -3, 1, 3, -1, -2), (-3, -2, 3, 0, 2, -1, 1)),
    ((0, 1, -1, 3, -2, 2, -3), (-2, 0, 2, -3, 1, -1, 3)),
)


def run_kernel(body, outs, args, specs=None, out_specs=None, scratch=(), flops=0):
    return pl.pallas_call(
        body,
        out_shape=[jax.ShapeDtypeStruct(shape, dtype) for shape, dtype in outs],
        in_specs=specs or [VMEM] * len(args),
        out_specs=out_specs or [VMEM] * len(outs),
        scratch_shapes=list(scratch),
        compiler_params=pltpu.CompilerParams(vmem_limit_bytes=12 * 2**20),
        cost_estimate=pl.CostEstimate(flops=flops, bytes_accessed=2**19, transcendentals=0),
    )(*args)


def rows_of(first, rows):
    return pl.ds(pl.multiple_of(first * rows, rows), rows)


def order_of(chips, second, phase):
    if 2 * chips - 1 == len(TURNS[0][0]):
        turns = TURNS[phase][int(second)]
    else:
        cross, plane = list(range(chips)), [-step for step in reversed(range(1, chips))]
        turns = plane + cross if second else cross + plane
    return [(int(turn >= 0), abs(turn)) for turn in turns]


def in_second():
    return 2 * lax.axis_index("low") >= lax.axis_size("low")


def turn_of(chips, turn, phase):
    second = in_second()
    return [
        jnp.where(second, late, soon)
        for soon, late in zip(order_of(chips, False, phase)[turn], order_of(chips, True, phase)[turn])
    ]


def pack_body(less, more, *refs):
    soon, (away, keep, held, turned, sems) = refs[:SOON], refs[SOON:]
    chip, core = lax.axis_index("chip"), lax.axis_index("core")
    copies = [
        pltpu.make_async_copy(source, held.at[place], sems.at[place])
        for place, source in enumerate((less, more))
    ]
    for copy in copies:
        copy.start()
    chips, _, _, rows, _ = away.shape
    for kind in range(2):
        copies[kind].wait()
        for part in range(2):
            whole = held[kind, part, 0]
            if kind == 0:
                whole = whole.astype(F32).T.astype(BF16)
            turned[kind, part] = whole
    for turn, block in enumerate(soon):
        crosses, step = turn_of(chips, turn, 0)
        for owner in range(2):
            block[owner] = turned[crosses, :, rows_of(2 * (chip ^ step) + owner, rows)]
    for kind in range(2):
        for place in range(chips):
            top = 2 * (chip ^ place)
            away[place, kind] = turned[kind, :, rows_of(top + 1 - core, rows)]
            keep[place, kind] = turned[kind, :, rows_of(top + core, rows)]


def pair_body(phase, keep, got, *blocks):
    chips, kinds = keep.shape[:2]
    for turn, block in enumerate(blocks, SOON):
        crosses, step = turn_of(chips, turn, phase)
        kind = crosses if kinds == 2 else 0
        block[0] = keep[step, kind]
        block[1] = got[step, kind]


def late_body(*refs):
    away = refs[-1]
    for turn in range(SOON):
        away[turn] = refs[turn][1 - lax.axis_index("core")]


def sort_blocks(chips, phase, blocks, late, put):
    core = lax.axis_index("core")
    for turn, block in enumerate(blocks):
        crosses, step = turn_of(chips, turn, phase)
        if turn < SOON:
            put(crosses, step, block[core], late[turn])
        else:
            put(crosses, step, block[0], block[1])


def lag_body(keep, got, late, *refs):
    blocks, soon = refs[: -4 - SOON], refs[-4 - SOON : -4]
    away, kept, joined, polar = refs[-4:]
    chip, core = lax.axis_index("chip"), lax.axis_index("core")
    energies, _, rows, width = polar.shape
    chips = energies // 2

    def put(crosses, step, mine, theirs):
        joined[2 * (chip ^ step) + core, crosses] = mine
        joined[2 * (chip ^ step) + 1 - core, crosses] = theirs

    put(0, 0, keep[0, 0], got[0, 0])
    sort_blocks(chips, 0, blocks, late, put)
    factor = energies ** (-0.5)
    for top in range(0, rows, 16):
        for left in range(0, width, 128):
            at = (pl.ds(top, 16), pl.ds(left, 128))
            for lag in range(energies):
                real = imag = jnp.zeros((16, 128), F32)
                for late in range(lag, energies):
                    lr = joined[(late, 0, 0) + at].astype(F32)
                    li = joined[(late, 0, 1) + at].astype(F32)
                    mr = joined[(late - lag, 1, 0) + at].astype(F32)
                    mi = joined[(late - lag, 1, 1) + at].astype(F32)
                    real += lr * mr - li * mi
                    imag += lr * mi + li * mr
                polar[(lag, 0) + at] = (factor * imag).astype(BF16)
                polar[(lag, 1) + at] = (-factor * real).astype(BF16)
    for turn, block in enumerate(soon):
        _, step = turn_of(chips, turn, 1)
        for owner in range(2):
            block[owner] = polar[2 * (chip ^ step) + owner]
    for place in range(chips):
        top = 2 * (chip ^ place)
        away[place, 0] = polar[top + 1 - core]
        kept[place, 0] = polar[top + core]


def across(left, turned):
    return lax.dot_general(
        left, turned, (((1,), (1,)), ((), ())), preferred_element_type=F32
    ).astype(BF16)


def weigh_body(blocks, onsite_scale, coupling_scale, mask, link, _, coupling, weights):
    row, col = blocks[0, 0], blocks[0, 1]
    low = jnp.minimum(row, col)
    strength = coupling_scale[low]
    weights[0] = jnp.full(weights.shape[1:], onsite_scale[row] * onsite_scale[col], F32)
    weights[1] = jnp.full(
        weights.shape[1:], mask[low, low + 1].astype(F32) * strength * strength, F32
    )

    @pl.when(row < col)
    def _():
        coupling[...] = link[...]

    @pl.when(row >= col)
    def _():
        coupling[...] = link[...].astype(F32).T.astype(BF16)


def screen_body(onsite, coupling, weights, keep, got, late, *refs):
    blocks = refs[:-4]
    out, whole, ready, sems = refs[-4:]
    chip, core = lax.axis_index("chip"), lax.axis_index("core")
    chips, _, _, rows, width = keep.shape

    def put(slot, step, mine, theirs):
        whole[slot, :, rows_of(2 * (chip ^ step) + core, rows)] = mine
        whole[slot, :, rows_of(2 * (chip ^ step) + 1 - core, rows)] = theirs

    put(0, 0, keep[0, 0], got[0, 0])
    sort_blocks(chips, 1, blocks, late, put)
    copies = []
    inner_own = across(onsite[...], whole[0].reshape(2 * width, width))
    inner_other = across(coupling[...], whole[1].reshape(2 * width, width))
    for part in range(2):
        at = slice(part * width, (part + 1) * width)
        term = weights[0, 0, 0] * jnp.dot(
            inner_own[:, at], onsite[...], preferred_element_type=F32
        )
        mirrored = weights[1, 0, 0] * jnp.dot(
            inner_other[:, at], coupling[...], preferred_element_type=F32
        )
        ready[part, 0] = (term + mirrored.astype(BF16).astype(F32)).astype(BF16)
        copies.append(pltpu.make_async_copy(ready.at[part], out.at[part], sems.at[part]))
        copies[-1].start()
    for copy in copies:
        copy.wait()


def on_device(
    green_less,
    green_greater,
    pair_blocks,
    onsite_scale,
    coupling_scale,
    coupling_mask,
    onsite_block,
    coupling_block,
):
    chips, lows = lax.axis_size("chip"), lax.axis_size("low")
    energies = 2 * chips
    width = green_less.shape[3]
    rows = width // energies

    def piles(kinds):
        return ((chips, kinds, 2, rows, width), BF16)

    block_shape = ((2, 2, rows, width), BF16)

    def swap_cores(value):
        return lax.ppermute(value, "core", [(0, 1), (1, 0)])

    def spread(soon, away, keep, phase):
        got = swap_cores(away)
        later = run_kernel(
            functools.partial(pair_body, phase), [block_shape] * (2 * chips - 1 - SOON), (keep, got)
        )
        came = []
        for turn, block in enumerate((*soon, *later)):
            pairs = []
            for chip in range(chips):
                for half in range(2):
                    for low in range(lows):
                        crosses, step = order_of(chips, 2 * low >= lows, phase)[turn]
                        source = (chip * 2 + half) * lows + low
                        target = ((chip ^ step) * 2 + (half ^ crosses)) * lows + low
                        pairs.append((source, target))
            came.append(lax.ppermute(block, ("chip", "half", "low"), pairs))
        (away,) = run_kernel(late_body, [((SOON, 2, rows, width), BF16)], (*came[:SOON], later[0], came[3]))
        return keep, got, swap_cores(away), *came

    *soon, away, keep = run_kernel(
        pack_body,
        [block_shape] * SOON + [piles(2)] * 2,
        [pltpu.with_memory_space_constraint(value, pltpu.HBM) for value in (green_less, green_greater)],
        specs=[HBM] * 2,
        scratch=[
            pltpu.VMEM((2, 2, 1, width, width), BF16),
            pltpu.VMEM((2, 2, width, width), BF16),
            pltpu.SemaphoreType.DMA((2,)),
        ],
    )
    *soon, away, keep = run_kernel(
        lag_body,
        [block_shape] * SOON + [piles(1)] * 2,
        spread(soon, away, keep, 0),
        scratch=[
            pltpu.VMEM((energies, 2, 2, rows, width), BF16),
            pltpu.VMEM((energies, 2, rows, width), BF16),
        ],
        flops=energies * (energies + 1) * 4 * rows * width,
    )
    parts = spread(soon, away, keep, 1)
    coupling, weights = run_kernel(
        weigh_body,
        [((width, width), BF16), ((2, 8, 128), F32)],
        (pair_blocks, onsite_scale, coupling_scale, coupling_mask, coupling_block, away),
        specs=[SMEM] * 4 + [VMEM] * 2,
    )
    (screened,) = run_kernel(
        screen_body,
        [((2, 1, width, width), BF16)],
        (onsite_block, coupling, weights, *parts),
        out_specs=[HBM],
        scratch=[
            pltpu.VMEM((2, 2, width, width), BF16),
            pltpu.VMEM((2, 1, width, width), BF16),
            pltpu.SemaphoreType.DMA((2,)),
        ],
        flops=16 * width**3,
    )
    return screened


def solution(mesh):
    energies, pairs = mesh.shape["energy"], mesh.shape["pair"]
    fine = Mesh(
        mesh.devices.reshape(energies // 2, 2, 2, pairs // 2), ("chip", "core", "half", "low")
    )
    across_mesh = P(None, ("chip", "core"), ("half", "low"), None)
    return jax.shard_map(
        on_device,
        mesh=fine,
        in_specs=(across_mesh, across_mesh, P(("half", "low"), None), P(), P(), P(), P(), P()),
        out_specs=across_mesh,
        check_vma=False,
    )
```

```python
import functools

import jax
import jax.numpy as jnp
from jax import lax
from jax.experimental import pallas as pl
from jax.experimental.pallas import tpu as pltpu
from jax.sharding import Mesh
from jax.sharding import PartitionSpec as P

BF16 = jnp.bfloat16
F32 = jnp.float32
VMEM = pl.BlockSpec(memory_space=pltpu.VMEM)
SMEM = pl.BlockSpec(memory_space=pltpu.SMEM)
HBM = pl.BlockSpec(memory_space=pltpu.HBM)
SOON = 2
TURNS = (
    ((0, 2, -3, 1, 3, -1, -2), (-3, -2, 3, 0, -1, 2, 1)),
    ((0, 1, -1, 3, -2, 2, -3), (-2, 0, 2, -3, -1, 1, 3)),
)


def run_kernel(body, outs, args, specs=None, out_specs=None, scratch=(), flops=0):
    return pl.pallas_call(
        body,
        out_shape=[jax.ShapeDtypeStruct(shape, dtype) for shape, dtype in outs],
        in_specs=specs or [VMEM] * len(args),
        out_specs=out_specs or [VMEM] * len(outs),
        scratch_shapes=list(scratch),
        compiler_params=pltpu.CompilerParams(vmem_limit_bytes=12 * 2**20),
        cost_estimate=pl.CostEstimate(flops=flops, bytes_accessed=2**19, transcendentals=0),
    )(*args)


def rows_of(first, rows):
    return pl.ds(pl.multiple_of(first * rows, rows), rows)


def order_of(chips, second, phase):
    if 2 * chips - 1 == len(TURNS[0][0]):
        turns = TURNS[phase][int(second)]
    else:
        cross, plane = list(range(chips)), [-step for step in reversed(range(1, chips))]
        turns = plane + cross if second else cross + plane
    return [(int(turn >= 0), abs(turn)) for turn in turns]


def in_second():
    return 2 * lax.axis_index("low") >= lax.axis_size("low")


def turn_of(chips, turn, phase):
    second = in_second()
    return [
        jnp.where(second, late, soon)
        for soon, late in zip(order_of(chips, False, phase)[turn], order_of(chips, True, phase)[turn])
    ]


def pack_body(less, more, *refs):
    soon, (away, keep, held, turned, sems) = refs[:SOON], refs[SOON:]
    chip, core = lax.axis_index("chip"), lax.axis_index("core")
    copies = [
        pltpu.make_async_copy(source, held.at[place], sems.at[place])
        for place, source in enumerate((less, more))
    ]
    for copy in copies:
        copy.start()
    chips, _, _, rows, _ = away.shape
    for kind in range(2):
        copies[kind].wait()
        for part in range(2):
            whole = held[kind, part, 0]
            if kind == 0:
                whole = whole.astype(F32).T.astype(BF16)
            turned[kind, part] = whole
    for turn, block in enumerate(soon):
        crosses, step = turn_of(chips, turn, 0)
        for owner in range(2):
            block[owner] = turned[crosses, :, rows_of(2 * (chip ^ step) + owner, rows)]
    for kind in range(2):
        for place in range(chips):
            top = 2 * (chip ^ place)
            away[place, kind] = turned[kind, :, rows_of(top + 1 - core, rows)]
            keep[place, kind] = turned[kind, :, rows_of(top + core, rows)]


def pair_body(phase, keep, got, *blocks):
    chips, kinds = keep.shape[:2]
    for turn, block in enumerate(blocks, SOON):
        crosses, step = turn_of(chips, turn, phase)
        kind = crosses if kinds == 2 else 0
        block[0] = keep[step, kind]
        block[1] = got[step, kind]


def late_body(*refs):
    away = refs[-1]
    for turn in range(SOON):
        away[turn] = refs[turn][1 - lax.axis_index("core")]


def sort_blocks(chips, phase, blocks, late, put):
    core = lax.axis_index("core")
    for turn, block in enumerate(blocks):
        crosses, step = turn_of(chips, turn, phase)
        if turn < SOON:
            put(crosses, step, block[core], late[turn])
        else:
            put(crosses, step, block[0], block[1])


def lag_body(_, keep, got, late, *refs):
    blocks, soon = refs[: -4 - SOON], refs[-4 - SOON : -4]
    away, kept, joined, polar = refs[-4:]
    chip, core = lax.axis_index("chip"), lax.axis_index("core")
    energies, _, rows, width = polar.shape
    chips = energies // 2

    def put(crosses, step, mine, theirs):
        joined[2 * (chip ^ step) + core, crosses] = mine
        joined[2 * (chip ^ step) + 1 - core, crosses] = theirs

    put(0, 0, keep[0, 0], got[0, 0])
    sort_blocks(chips, 0, blocks, late, put)
    factor = energies ** (-0.5)
    for top in range(0, rows, 16):
        for left in range(0, width, 128):
            at = (pl.ds(top, 16), pl.ds(left, 128))
            for lag in range(energies):
                real = imag = jnp.zeros((16, 128), F32)
                for late in range(lag, energies):
                    lr = joined[(late, 0, 0) + at].astype(F32)
                    li = joined[(late, 0, 1) + at].astype(F32)
                    mr = joined[(late - lag, 1, 0) + at].astype(F32)
                    mi = joined[(late - lag, 1, 1) + at].astype(F32)
                    real += lr * mr - li * mi
                    imag += lr * mi + li * mr
                polar[(lag, 0) + at] = (factor * imag).astype(BF16)
                polar[(lag, 1) + at] = (-factor * real).astype(BF16)
    for turn, block in enumerate(soon):
        _, step = turn_of(chips, turn, 1)
        for owner in range(2):
            block[owner] = polar[2 * (chip ^ step) + owner]
    for place in range(chips):
        top = 2 * (chip ^ place)
        away[place, 0] = polar[top + 1 - core]
        kept[place, 0] = polar[top + core]


def across(left, turned):
    return lax.dot_general(
        left, turned, (((1,), (1,)), ((), ())), preferred_element_type=F32
    ).astype(BF16)


def weigh_body(blocks, onsite_scale, coupling_scale, mask, link, _, coupling, weights):
    row, col = blocks[0, 0], blocks[0, 1]
    low = jnp.minimum(row, col)
    strength = coupling_scale[low]
    weights[0] = jnp.full(weights.shape[1:], onsite_scale[row] * onsite_scale[col], F32)
    weights[1] = jnp.full(
        weights.shape[1:], mask[low, low + 1].astype(F32) * strength * strength, F32
    )

    @pl.when(row < col)
    def _():
        coupling[...] = link[...]

    @pl.when(row >= col)
    def _():
        coupling[...] = link[...].astype(F32).T.astype(BF16)


def screen_body(onsite, coupling, weights, keep, got, late, *refs):
    blocks = refs[:-4]
    out, whole, ready, sems = refs[-4:]
    chip, core = lax.axis_index("chip"), lax.axis_index("core")
    chips, _, _, rows, width = keep.shape

    def put(slot, step, mine, theirs):
        whole[slot, :, rows_of(2 * (chip ^ step) + core, rows)] = mine
        whole[slot, :, rows_of(2 * (chip ^ step) + 1 - core, rows)] = theirs

    put(0, 0, keep[0, 0], got[0, 0])
    sort_blocks(chips, 1, blocks, late, put)
    copies = []
    inner_own = across(onsite[...], whole[0].reshape(2 * width, width))
    inner_other = across(coupling[...], whole[1].reshape(2 * width, width))
    for part in range(2):
        at = slice(part * width, (part + 1) * width)
        term = weights[0, 0, 0] * jnp.dot(
            inner_own[:, at], onsite[...], preferred_element_type=F32
        )
        mirrored = weights[1, 0, 0] * jnp.dot(
            inner_other[:, at], coupling[...], preferred_element_type=F32
        )
        ready[part, 0] = (term + mirrored.astype(BF16).astype(F32)).astype(BF16)
        copies.append(pltpu.make_async_copy(ready.at[part], out.at[part], sems.at[part]))
        copies[-1].start()
    for copy in copies:
        copy.wait()


def on_device(
    green_less,
    green_greater,
    pair_blocks,
    onsite_scale,
    coupling_scale,
    coupling_mask,
    onsite_block,
    coupling_block,
):
    chips, lows = lax.axis_size("chip"), lax.axis_size("low")
    energies = 2 * chips
    width = green_less.shape[3]
    rows = width // energies

    def piles(kinds):
        return ((chips, kinds, 2, rows, width), BF16)

    block_shape = ((2, 2, rows, width), BF16)

    def swap_cores(value):
        return lax.ppermute(value, "core", [(0, 1), (1, 0)])

    def spread(soon, away, keep, phase):
        got = swap_cores(away)
        later = run_kernel(
            functools.partial(pair_body, phase), [block_shape] * (2 * chips - 1 - SOON), (keep, got)
        )
        came = []
        for turn, block in enumerate((*soon, *later)):
            pairs = []
            for chip in range(chips):
                for half in range(2):
                    for low in range(lows):
                        crosses, step = order_of(chips, 2 * low >= lows, phase)[turn]
                        source = (chip * 2 + half) * lows + low
                        target = ((chip ^ step) * 2 + (half ^ crosses)) * lows + low
                        pairs.append((source, target))
            came.append(lax.ppermute(block, ("chip", "half", "low"), pairs))
        (away,) = run_kernel(late_body, [((SOON, 2, rows, width), BF16)], (*came[:SOON], later[0], came[3]))
        return keep, got, swap_cores(away), *came

    *soon, away, keep = run_kernel(
        pack_body,
        [block_shape] * SOON + [piles(2)] * 2,
        [pltpu.with_memory_space_constraint(value, pltpu.HBM) for value in (green_less, green_greater)],
        specs=[HBM] * 2,
        scratch=[
            pltpu.VMEM((2, 2, 1, width, width), BF16),
            pltpu.VMEM((2, 2, width, width), BF16),
            pltpu.SemaphoreType.DMA((2,)),
        ],
    )
    coupling, weights = run_kernel(
        weigh_body,
        [((width, width), BF16), ((2, 8, 128), F32)],
        (pair_blocks, onsite_scale, coupling_scale, coupling_mask, coupling_block, keep),
        specs=[SMEM] * 4 + [VMEM] * 2,
    )
    *soon, away, keep = run_kernel(
        lag_body,
        [block_shape] * SOON + [piles(1)] * 2,
        (weights, *spread(soon, away, keep, 0)),
        scratch=[
            pltpu.VMEM((energies, 2, 2, rows, width), BF16),
            pltpu.VMEM((energies, 2, rows, width), BF16),
        ],
        flops=energies * (energies + 1) * 4 * rows * width,
    )
    parts = spread(soon, away, keep, 1)
    (screened,) = run_kernel(
        screen_body,
        [((2, 1, width, width), BF16)],
        (onsite_block, coupling, weights, *parts),
        out_specs=[HBM],
        scratch=[
            pltpu.VMEM((2, 2, width, width), BF16),
            pltpu.VMEM((2, 1, width, width), BF16),
            pltpu.SemaphoreType.DMA((2,)),
        ],
        flops=16 * width**3,
    )
    return screened


def solution(mesh):
    energies, pairs = mesh.shape["energy"], mesh.shape["pair"]
    fine = Mesh(
        mesh.devices.reshape(energies // 2, 2, 2, pairs // 2), ("chip", "core", "half", "low")
    )
    across_mesh = P(None, ("chip", "core"), ("half", "low"), None)
    return jax.shard_map(
        on_device,
        mesh=fine,
        in_specs=(across_mesh, across_mesh, P(("half", "low"), None), P(), P(), P(), P(), P()),
        out_specs=across_mesh,
        check_vma=False,
    )
```

```python
import functools

import jax
import jax.numpy as jnp
from jax import lax
from jax.experimental import pallas as pl
from jax.experimental.pallas import tpu as pltpu
from jax.sharding import Mesh
from jax.sharding import PartitionSpec as P

BF16 = jnp.bfloat16
F32 = jnp.float32
VMEM = pl.BlockSpec(memory_space=pltpu.VMEM)
SMEM = pl.BlockSpec(memory_space=pltpu.SMEM)
HBM = pl.BlockSpec(memory_space=pltpu.HBM)
SOON = 2
TURNS = (
    ((0, 2, -3, 1, 3, -1, -2), (-3, -2, 3, 0, -1, 2, 1)),
    ((0, 1, -1, 3, -2, 2, -3), (-2, 0, 2, -3, -1, 1, 3)),
)


def run_kernel(body, outs, args, specs=None, out_specs=None, scratch=(), flops=0):
    return pl.pallas_call(
        body,
        out_shape=[jax.ShapeDtypeStruct(shape, dtype) for shape, dtype in outs],
        in_specs=specs or [VMEM] * len(args),
        out_specs=out_specs or [VMEM] * len(outs),
        scratch_shapes=list(scratch),
        compiler_params=pltpu.CompilerParams(vmem_limit_bytes=12 * 2**20),
        cost_estimate=pl.CostEstimate(flops=flops, bytes_accessed=2**19, transcendentals=0),
    )(*args)


def rows_of(first, rows):
    return pl.ds(pl.multiple_of(first * rows, rows), rows)


def order_of(chips, second, phase):
    if 2 * chips - 1 == len(TURNS[0][0]):
        turns = TURNS[phase][int(second)]
    else:
        cross, plane = list(range(chips)), [-step for step in reversed(range(1, chips))]
        turns = plane + cross if second else cross + plane
    return [(int(turn >= 0), abs(turn)) for turn in turns]


def in_second():
    return 2 * lax.axis_index("low") >= lax.axis_size("low")


def turn_of(chips, turn, phase):
    second = in_second()
    return [
        jnp.where(second, late, soon)
        for soon, late in zip(order_of(chips, False, phase)[turn], order_of(chips, True, phase)[turn])
    ]


def pack_body(less, more, *refs):
    soon, (away, keep, held, turned, sems) = refs[:SOON], refs[SOON:]
    chip, core = lax.axis_index("chip"), lax.axis_index("core")
    copies = [
        pltpu.make_async_copy(source, held.at[place], sems.at[place])
        for place, source in enumerate((less, more))
    ]
    for copy in copies:
        copy.start()
    chips, _, _, rows, _ = away.shape
    for kind in range(2):
        copies[kind].wait()
        for part in range(2):
            whole = held[kind, part, 0]
            if kind == 0:
                whole = whole.astype(F32).T.astype(BF16)
            turned[kind, part] = whole
    for turn, block in enumerate(soon):
        crosses, step = turn_of(chips, turn, 0)
        for owner in range(2):
            block[owner] = turned[crosses, :, rows_of(2 * (chip ^ step) + owner, rows)]
    for kind in range(2):
        for place in range(chips):
            top = 2 * (chip ^ place)
            away[place, kind] = turned[kind, :, rows_of(top + 1 - core, rows)]
            keep[place, kind] = turned[kind, :, rows_of(top + core, rows)]


def pair_body(phase, keep, got, *blocks):
    chips, kinds = keep.shape[:2]
    for turn, block in enumerate(blocks, SOON):
        crosses, step = turn_of(chips, turn, phase)
        kind = crosses if kinds == 2 else 0
        block[0] = keep[step, kind]
        block[1] = got[step, kind]


def late_body(*refs):
    away = refs[-1]
    for turn in range(SOON):
        away[turn] = refs[turn][1 - lax.axis_index("core")]


def sort_blocks(chips, phase, blocks, late, put):
    core = lax.axis_index("core")
    for turn, block in enumerate(blocks):
        crosses, step = turn_of(chips, turn, phase)
        if turn < SOON:
            put(crosses, step, block[core], late[turn])
        else:
            put(crosses, step, block[0], block[1])


def lag_body(_, keep, got, late, *refs):
    blocks, soon = refs[: -4 - SOON], refs[-4 - SOON : -4]
    away, kept, joined, polar = refs[-4:]
    chip, core = lax.axis_index("chip"), lax.axis_index("core")
    energies, _, rows, width = polar.shape
    chips = energies // 2

    def put(crosses, step, mine, theirs):
        joined[2 * (chip ^ step) + core, crosses] = mine.astype(F32)
        joined[2 * (chip ^ step) + 1 - core, crosses] = theirs.astype(F32)

    put(0, 0, keep[0, 0], got[0, 0])
    sort_blocks(chips, 0, blocks, late, put)
    factor = energies ** (-0.5)
    for top in range(0, rows, 16):
        for left in range(0, width, 128):
            at = (pl.ds(top, 16), pl.ds(left, 128))
            for lag in range(energies):
                real = imag = jnp.zeros((16, 128), F32)
                for late in range(lag, energies):
                    lr = joined[(late, 0, 0) + at]
                    li = joined[(late, 0, 1) + at]
                    mr = joined[(late - lag, 1, 0) + at]
                    mi = joined[(late - lag, 1, 1) + at]
                    real += lr * mr - li * mi
                    imag += lr * mi + li * mr
                polar[(lag, 0) + at] = (factor * imag).astype(BF16)
                polar[(lag, 1) + at] = (-factor * real).astype(BF16)
    for turn, block in enumerate(soon):
        _, step = turn_of(chips, turn, 1)
        for owner in range(2):
            block[owner] = polar[2 * (chip ^ step) + owner]
    for place in range(chips):
        top = 2 * (chip ^ place)
        away[place, 0] = polar[top + 1 - core]
        kept[place, 0] = polar[top + core]


def across(left, turned):
    return lax.dot_general(
        left, turned, (((1,), (1,)), ((), ())), preferred_element_type=F32
    ).astype(BF16)


def weigh_body(blocks, onsite_scale, coupling_scale, mask, link, _, coupling, weights):
    row, col = blocks[0, 0], blocks[0, 1]
    low = jnp.minimum(row, col)
    strength = coupling_scale[low]
    weights[0] = jnp.full(weights.shape[1:], onsite_scale[row] * onsite_scale[col], F32)
    weights[1] = jnp.full(
        weights.shape[1:], mask[low, low + 1].astype(F32) * strength * strength, F32
    )

    @pl.when(row < col)
    def _():
        coupling[...] = link[...]

    @pl.when(row >= col)
    def _():
        coupling[...] = link[...].astype(F32).T.astype(BF16)


def screen_body(onsite, coupling, weights, keep, got, late, *refs):
    blocks = refs[:-4]
    out, whole, ready, sems = refs[-4:]
    chip, core = lax.axis_index("chip"), lax.axis_index("core")
    chips, _, _, rows, width = keep.shape

    def put(slot, step, mine, theirs):
        whole[slot, :, rows_of(2 * (chip ^ step) + core, rows)] = mine
        whole[slot, :, rows_of(2 * (chip ^ step) + 1 - core, rows)] = theirs

    put(0, 0, keep[0, 0], got[0, 0])
    sort_blocks(chips, 1, blocks, late, put)
    copies = []
    inner_own = across(onsite[...], whole[0].reshape(2 * width, width))
    inner_other = across(coupling[...], whole[1].reshape(2 * width, width))
    for part in range(2):
        at = slice(part * width, (part + 1) * width)
        term = weights[0, 0, 0] * jnp.dot(
            inner_own[:, at], onsite[...], preferred_element_type=F32
        )
        mirrored = weights[1, 0, 0] * jnp.dot(
            inner_other[:, at], coupling[...], preferred_element_type=F32
        )
        ready[part, 0] = (term + mirrored.astype(BF16).astype(F32)).astype(BF16)
        copies.append(pltpu.make_async_copy(ready.at[part], out.at[part], sems.at[part]))
        copies[-1].start()
    for copy in copies:
        copy.wait()


def on_device(
    green_less,
    green_greater,
    pair_blocks,
    onsite_scale,
    coupling_scale,
    coupling_mask,
    onsite_block,
    coupling_block,
):
    chips, lows = lax.axis_size("chip"), lax.axis_size("low")
    energies = 2 * chips
    width = green_less.shape[3]
    rows = width // energies

    def piles(kinds):
        return ((chips, kinds, 2, rows, width), BF16)

    block_shape = ((2, 2, rows, width), BF16)

    def swap_cores(value):
        return lax.ppermute(value, "core", [(0, 1), (1, 0)])

    def spread(soon, away, keep, phase):
        got = swap_cores(away)
        later = run_kernel(
            functools.partial(pair_body, phase), [block_shape] * (2 * chips - 1 - SOON), (keep, got)
        )
        came = []
        for turn, block in enumerate((*soon, *later)):
            pairs = []
            for chip in range(chips):
                for half in range(2):
                    for low in range(lows):
                        crosses, step = order_of(chips, 2 * low >= lows, phase)[turn]
                        source = (chip * 2 + half) * lows + low
                        target = ((chip ^ step) * 2 + (half ^ crosses)) * lows + low
                        pairs.append((source, target))
            came.append(lax.ppermute(block, ("chip", "half", "low"), pairs))
        (away,) = run_kernel(late_body, [((SOON, 2, rows, width), BF16)], (*came[:SOON], later[0], came[3]))
        return keep, got, swap_cores(away), *came

    *soon, away, keep = run_kernel(
        pack_body,
        [block_shape] * SOON + [piles(2)] * 2,
        [pltpu.with_memory_space_constraint(value, pltpu.HBM) for value in (green_less, green_greater)],
        specs=[HBM] * 2,
        scratch=[
            pltpu.VMEM((2, 2, 1, width, width), BF16),
            pltpu.VMEM((2, 2, width, width), BF16),
            pltpu.SemaphoreType.DMA((2,)),
        ],
    )
    coupling, weights = run_kernel(
        weigh_body,
        [((width, width), BF16), ((2, 8, 128), F32)],
        (pair_blocks, onsite_scale, coupling_scale, coupling_mask, coupling_block, keep),
        specs=[SMEM] * 4 + [VMEM] * 2,
    )
    *soon, away, keep = run_kernel(
        lag_body,
        [block_shape] * SOON + [piles(1)] * 2,
        (weights, *spread(soon, away, keep, 0)),
        scratch=[
            pltpu.VMEM((energies, 2, 2, rows, width), F32),
            pltpu.VMEM((energies, 2, rows, width), BF16),
        ],
        flops=energies * (energies + 1) * 4 * rows * width,
    )
    parts = spread(soon, away, keep, 1)
    (screened,) = run_kernel(
        screen_body,
        [((2, 1, width, width), BF16)],
        (onsite_block, coupling, weights, *parts),
        out_specs=[HBM],
        scratch=[
            pltpu.VMEM((2, 2, width, width), BF16),
            pltpu.VMEM((2, 1, width, width), BF16),
            pltpu.SemaphoreType.DMA((2,)),
        ],
        flops=16 * width**3,
    )
    return screened


def solution(mesh):
    energies, pairs = mesh.shape["energy"], mesh.shape["pair"]
    fine = Mesh(
        mesh.devices.reshape(energies // 2, 2, 2, pairs // 2), ("chip", "core", "half", "low")
    )
    across_mesh = P(None, ("chip", "core"), ("half", "low"), None)
    return jax.shard_map(
        on_device,
        mesh=fine,
        in_specs=(across_mesh, across_mesh, P(("half", "low"), None), P(), P(), P(), P(), P()),
        out_specs=across_mesh,
        check_vma=False,
    )
```
